512 devices in a mesh: pipe: 2 (over core), expert: 64 (over y, z), dp: 4 (over x).
Axes of the slice: x: 4, y: 4, z: 16, core: 2. Of those that a mesh axis runs over, the one named last changes fastest.
Arguments:
- tokens: bfloat16 [2, 2048, 3584], P('pipe', ('expert', 'dp')), may hold values from -6 to 6
- grad_out: bfloat16 [2, 2048, 3584], P('pipe', ('expert', 'dp')), may hold values from -1.5 to 1.5
- routes: int32 [2, 2048, 4], P('pipe', ('expert', 'dp')), may hold values from 0 to 7, all different within a row; in each aligned block of 8 rows (0 to 7, 8 to 15, ..., all dimensions but the last counted through in order) at most 6 rows name the same one
- combine: bfloat16 [2, 2048, 4], P('pipe', ('expert', 'dp')), may hold values from 0.25 to 2.5
- w_gate: bfloat16 [2, 3584, 8192], P('pipe', 'dp', 'expert'), may hold values from -0.09375 to 0.09375
- w_up: bfloat16 [2, 3584, 8192], P('pipe', 'dp', 'expert'), may hold values from -0.09375 to 0.09375
- w_down: bfloat16 [2, 3584, 8192], P('pipe', 'dp', 'expert'), may hold values from -0.1875 to 0.1875
Outputs:
- passed: bfloat16 [2, 2048, 3584], P('pipe', ('expert', 'dp'))
- grad_combine: float32 [2, 2048, 4], P('pipe', ('expert', 'dp'))
- grad_gate: float32 [2, 3584, 8192], P('pipe', 'dp', 'expert')
- grad_up: float32 [2, 3584, 8192], P('pipe', 'dp', 'expert')
- grad_down: float32 [2, 3584, 8192], P('pipe', 'dp', 'expert')
The draws below stay inside these ranges and needn't reach their ends.
Inputs may be any that keep to these rules, and one draw needn't show every extreme that they name: `routes`: each token names 4 different experts; among the 8 tokens of one device no expert is named more than 6 times, and in some device's tokens an expert is named exactly 6 times.
All inputs are finite; a program needn't handle non-finite values.
Results may differ from the reference program's by a relative error of at most 0.012.
Values may be sent and summed in bfloat16 or wider, within the bound.
No kernel may reach another device: no remote copies, remote signals or barrier semaphores. Data moves between devices by JAX's collectives and lax.ppermute only.
A program may use at most 128 MiB of HBM per device.

```python
import math
import jax
import jax.numpy as jnp
import numpy as np
from jax import lax

D = 3584
TOK_DEV = 8
SECTIONS = 2
GROUPS = 4
FF = 1024
EXPERTS = 8
TOP = 4
CAP = 6
TOKENS = 2048
N_EXPERT = 64


def steps_of(stream_key, extent, split, smallest, top_value):
    factor_of, own = 1.0, jax.random.fold_in(stream_key, 6)
    for axis_at, parts in split:
        steps = jnp.exp(jax.random.uniform(jax.random.fold_in(own, axis_at), (parts,), jnp.float32, smallest / len(split), top_value / len(split)))
        factor_of = factor_of * jnp.repeat(steps, extent[axis_at] // parts).reshape([-1 if axis == axis_at else 1 for axis in range(len(extent))])
    return factor_of


def routed_block(rng, own, number, rows, amount, top, most, lean):
    order = jax.random.permutation(rng, amount)
    crowded, common = load_shares(amount, rows * top, most, lean, True), load_shares(amount, rows * top, most, lean, False)
    places = jnp.arange(amount)

    def named(sizes, turn):
        used = int((sizes > 0).sum())
        fixed = max(1, used // 4)
        moved = fixed + (places - fixed + turn * (used - fixed)) % max(1, amount - fixed)
        return jnp.zeros((amount,), jnp.int32).at[order[jnp.where(places < fixed, places, moved)]].set(jnp.asarray(sizes, jnp.int32))

    sizes = jnp.where(number % 4 == 0, named(crowded, number // 4), named(common, number - number // 4 - 1))
    mixed = jax.random.permutation(jax.random.fold_in(own, 3), amount)
    donor, taker = mixed[0:amount // 2 * 2:2], mixed[1:amount // 2 * 2:2]
    slack = jnp.minimum(sizes[donor] - 1, most - sizes[taker]) // 2
    slack = jnp.where((donor == order[0]) | (taker == order[0]) | (sizes[taker] == 0), 0, jnp.maximum(slack, 0))
    moved = jax.random.randint(jax.random.fold_in(own, 4), (amount // 2,), 0, 1 << 20) % (slack + 1)
    sizes = sizes.at[donor].add(-moved).at[taker].add(moved)
    labels = jnp.searchsorted(jnp.cumsum(sizes), jnp.arange(rows * top), side="right").astype(jnp.int32)
    table = labels.reshape(top, rows).T
    table = table[jax.random.permutation(jax.random.fold_in(own, 1), rows)]
    turn = jax.random.randint(jax.random.fold_in(own, 2), (rows, 1), 0, top)
    return jnp.take_along_axis(table, (jnp.arange(top)[None, :] + turn) % top, axis=1)


def load_shares(amount, total, reach, lean, full):
    loads = [(1 << 20) // math.isqrt(standing ** lean) + 1 for standing in range(1, amount + 1)]
    largest = reach if full else min(reach, max(-(-total // amount), total * loads[0] // sum(loads)))
    least = 1 if total - largest >= amount - 1 else 0
    holding, rest = [largest] + [least] * (amount - 1), total - largest - least * (amount - 1)
    while rest > 0:
        movable = [i for i in range(1, amount) if holding[i] < largest] or [i for i in range(1, amount) if holding[i] < reach]
        whole, left = sum([loads[i] for i in movable]), rest
        for i in movable:
            more = min(reach - holding[i], max(1, left * loads[i] // whole), rest)
            holding[i] = holding[i] + more
            rest = rest - more
    return np.array(holding)


def normal_values(rng, shape, spread, limit, split=(), kind=jnp.bfloat16):
    level = steps_of(rng, shape, split, -0.22, 0.18) if split else 1.0
    array = jax.random.normal(rng, shape, jnp.float32) * spread * level
    return jnp.minimum(jnp.maximum(array, -limit), limit).astype(kind)


def setup_inputs(seed: int = 0) -> dict:
    streams_of = jax.random.split(jax.random.key(seed), 8)
    tokens = normal_values(streams_of[0], (SECTIONS, TOKENS, D), 1.0, 6.0, ((0, 2), (1, 256)))
    grad_out = normal_values(streams_of[1], (SECTIONS, TOKENS, D), 0.25, 1.5, ((0, 2), (1, 256)))
    routes_keys = jax.random.split(jax.random.fold_in(streams_of[2], 1), SECTIONS * TOKENS // TOK_DEV)
    routes_turns = jax.random.permutation(jax.random.fold_in(streams_of[2], 3), SECTIONS * TOKENS // TOK_DEV)
    routes = jax.vmap(lambda own, number: routed_block(jax.random.fold_in(streams_of[2], 2), own, number, TOK_DEV, EXPERTS, TOP, CAP, 2))(routes_keys, routes_turns).reshape((SECTIONS, TOKENS, TOP))
    combine = jnp.clip(jnp.exp(math.log(2.5) - 2.3025851 * jax.random.uniform(streams_of[3], (SECTIONS, TOKENS, TOP), jnp.float32) ** steps_of(streams_of[3], (SECTIONS, TOKENS, TOP), ((0, 2), (1, 256)), -0.2, 0.2)), 0.25, 2.5).astype(jnp.bfloat16)
    w_gate = normal_values(streams_of[4], (SECTIONS, D, EXPERTS * FF), D ** -0.5, 0.09375, ((0, 2), (1, 4), (2, 64)))
    w_up = normal_values(streams_of[5], (SECTIONS, D, EXPERTS * FF), D ** -0.5, 0.09375, ((0, 2), (1, 4), (2, 64)))
    w_down = normal_values(streams_of[6], (SECTIONS, D, EXPERTS * FF), FF ** -0.5, 0.1875, ((0, 2), (1, 4), (2, 64)))
    return {"tokens": tokens, "grad_out": grad_out, "routes": routes, "combine": combine, "w_gate": w_gate, "w_up": w_up, "w_down": w_down}


contract_last = (((1,), (1,)), ((), ()))
contract_first = (((0,), (0,)), ((), ()))


def expert_pass(row_inputs, row_cotangent, row_weight, gate_mat, up_mat, down_mat):
    gate_pre = jnp.dot(row_inputs, gate_mat, preferred_element_type=jnp.float32)
    up_pre = jnp.dot(row_inputs, up_mat, preferred_element_type=jnp.float32)
    sigmoid_gate = jax.nn.sigmoid(gate_pre)
    activated = gate_pre * sigmoid_gate
    hidden = (activated * up_pre).astype(jnp.bfloat16)
    expert_out = lax.dot_general(hidden, down_mat, contract_last, preferred_element_type=jnp.float32)
    route_score = jnp.sum(expert_out * row_cotangent.astype(jnp.float32), axis=1)
    out_grad = (row_weight[:, None] * row_cotangent.astype(jnp.float32)).astype(jnp.bfloat16)
    hidden_grad = jnp.dot(out_grad, down_mat, preferred_element_type=jnp.float32)
    gate_grad = (hidden_grad * up_pre * sigmoid_gate * (1.0 + gate_pre * (1.0 - sigmoid_gate))).astype(jnp.bfloat16)
    up_grad = (hidden_grad * activated).astype(jnp.bfloat16)
    input_grad = lax.dot_general(gate_grad, gate_mat, contract_last, preferred_element_type=jnp.float32)
    input_grad = input_grad + lax.dot_general(up_grad, up_mat, contract_last, preferred_element_type=jnp.float32)
    return route_score, input_grad, gate_grad, up_grad, out_grad, hidden


def group_sums(first_factor, second_factor):
    first_groups = first_factor.reshape(N_EXPERT, GROUPS, TOK_DEV, first_factor.shape[1])
    second_groups = second_factor.reshape(N_EXPERT, GROUPS, TOK_DEV, second_factor.shape[1])
    summed = jnp.zeros((first_factor.shape[1], second_factor.shape[1]), jnp.float32)
    for group_index in range(GROUPS):
        first_rows = first_groups[:, group_index].reshape(N_EXPERT * TOK_DEV, first_factor.shape[1])
        second_rows = second_groups[:, group_index].reshape(N_EXPERT * TOK_DEV, second_factor.shape[1])
        partial_value = lax.dot_general(first_rows, second_rows, contract_first, preferred_element_type=jnp.float32)
        rounded = lax.optimization_barrier(partial_value.astype(jnp.bfloat16))
        summed = summed + rounded.astype(jnp.float32)
    return summed


def one_section(section_tokens, section_cotangent, section_routes, section_combine, gate_all, up_all, down_all):
    weights_float = section_combine.astype(jnp.float32)

    def one_expert(carry, expert_index):
        gate_mat = lax.dynamic_slice_in_dim(gate_all, expert_index * FF, FF, 1)
        up_mat = lax.dynamic_slice_in_dim(up_all, expert_index * FF, FF, 1)
        down_mat = lax.dynamic_slice_in_dim(down_all, expert_index * FF, FF, 1)
        chosen = section_routes == expert_index
        row_weight = jnp.sum(jnp.where(chosen, weights_float, 0.0), axis=1)
        route_score, input_grad, gate_grad, up_grad, out_grad, hidden = expert_pass(
            section_tokens, section_cotangent, row_weight, gate_mat, up_mat, down_mat)
        new_carry = (carry[0] + input_grad, carry[1] + jnp.where(chosen, route_score[:, None], 0.0))
        grad_sums = (group_sums(section_tokens, gate_grad), group_sums(section_tokens, up_grad), group_sums(out_grad, hidden))
        return new_carry, grad_sums

    start_carry = (jnp.zeros((TOKENS, D), jnp.float32), jnp.zeros((TOKENS, TOP), jnp.float32))
    final_carry, stacked = lax.scan(one_expert, start_carry, jnp.arange(EXPERTS, dtype=jnp.int32))

    def arrange(stacked_grads):
        return jnp.transpose(stacked_grads, (1, 0, 2)).reshape(D, EXPERTS * FF)

    return final_carry[0], final_carry[1], arrange(stacked[0]), arrange(stacked[1]), arrange(stacked[2])


def reference(tokens, grad_out, routes, combine, w_gate, w_up, w_down):
    input_grads = []
    route_grads = []
    gate_grads = []
    up_grads = []
    down_grads = []
    for section_index in range(SECTIONS):
        results = one_section(tokens[section_index], grad_out[section_index], routes[section_index], combine[section_index],
                            w_gate[section_index], w_up[section_index], w_down[section_index])
        input_grads.append(results[0])
        route_grads.append(results[1])
        gate_grads.append(results[2])
        up_grads.append(results[3])
        down_grads.append(results[4])
    passed = jnp.stack([input_grads[(section_index + 1) % SECTIONS] for section_index in range(SECTIONS)]).astype(jnp.bfloat16)
    return passed, jnp.stack(route_grads), jnp.stack(gate_grads), jnp.stack(up_grads), jnp.stack(down_grads)
```

```python
import jax
import jax.numpy as jnp
from jax import lax
from jax.sharding import PartitionSpec as P

BF16 = jnp.bfloat16
F32 = jnp.float32
contract_first = (((0,), (0,)), ((), ()))
contract_last = (((1,), (1,)), ((), ()))


def exchange(blocks, axis, groups=None):
    return lax.all_to_all(blocks, axis, 0, 0, axis_index_groups=groups, tiled=True)


def body(tokens, grad_out, routes, combine, w_gate, w_up, w_down):
    tok, width = tokens.shape[1:]
    experts = 8
    n_x = lax.axis_size("dp")
    n_e = lax.axis_size("expert")
    n_z = 2 * (n_e // experts)
    n_y = n_e // n_z
    q = 4
    r = n_z // q
    cols = width // n_x
    ff = w_gate.shape[2]
    rows = n_z * n_x * tok
    along_y = [[y * n_z + z for y in range(n_y)] for z in range(n_z)]
    along_z = [[y * n_z + z for z in range(n_z)] for y in range(n_y)]
    near_z = [[y * n_z + a * r + b for b in range(r)] for y in range(n_y) for a in range(q)]
    far_z = [[y * n_z + a * r + b for a in range(q)] for y in range(n_y) for b in range(r)]
    upper_half = lax.axis_index("expert") % n_z >= n_z // 2

    own_weights = jnp.concatenate([w_gate[0], w_up[0], w_down[0]], axis=1)
    weights = lax.all_gather(own_weights, "expert", axis_index_groups=along_y)

    both = jnp.concatenate([tokens[0], grad_out[0]], axis=0).reshape(2 * tok, n_x, cols)
    both = exchange(both.transpose(1, 0, 2), "dp")
    x_rows = both[:, :tok].reshape(n_x * tok, cols)
    g_rows = both[:, tok:].reshape(n_x * tok, cols)
    chosen = routes[0][:, :, None] == jnp.arange(experts, dtype=jnp.int32)
    dense = jnp.sum(jnp.where(chosen, combine[0].astype(F32)[:, :, None], 0.0), axis=1)
    dense = jnp.pad(dense.astype(BF16), ((0, (n_x - 1) * tok), (0, 0)))
    g_rows = jnp.concatenate([g_rows, dense], axis=1)
    x_all = lax.all_gather(x_rows, "expert", axis_index_groups=along_z, tiled=True)
    g_all = lax.all_gather(g_rows, "expert", axis_index_groups=along_z, tiled=True)
    route_weight = g_all.reshape(n_z, n_x * tok, -1)[:, :tok, cols:].astype(F32)
    route_weight = route_weight.reshape(n_z * tok, n_y, 2)
    route_weight = jnp.where(upper_half, route_weight[:, :, 1], route_weight[:, :, 0])
    route_weight = route_weight.T[:, :, None]
    g_all = g_all[:, :cols]

    partial = []
    for y in range(n_y):
        first = jnp.dot(x_all, weights[y, :, : 2 * ff], preferred_element_type=F32)
        second = jnp.dot(g_all, weights[y, :, 2 * ff :], preferred_element_type=F32)
        partial.append(jnp.concatenate([first.astype(BF16), second.astype(BF16)], axis=1))
    partial = jnp.stack(partial).reshape(n_y, n_z, n_x, tok, 3 * ff).transpose(2, 0, 1, 3, 4)
    partial = exchange(partial, "dp")
    full = jnp.sum(partial.astype(F32), axis=0).reshape(n_y, n_z * tok, 3 * ff)
    gate = full[:, :, :ff]
    up = full[:, :, ff : 2 * ff]
    down_grad = full[:, :, 2 * ff :]
    sig = jax.nn.sigmoid(gate)
    act = gate * sig
    hidden = act * up
    score = jnp.sum(hidden * down_grad, axis=2)
    hidden_grad = down_grad * route_weight
    gate_grad = hidden_grad * up * sig * (1.0 + gate * (1.0 - sig))
    up_grad = hidden_grad * act
    grads = jnp.concatenate(
        [gate_grad.astype(BF16), up_grad.astype(BF16), (hidden * route_weight).astype(BF16)], axis=2
    )
    grads = exchange(jnp.broadcast_to(grads[None], (n_x,) + grads.shape), "dp")
    grads = grads.reshape(n_x, n_y, n_z, tok, 3 * ff).transpose(1, 2, 0, 3, 4)
    grads = grads.reshape(n_y, rows, 3 * ff)

    weight_grads = []
    for y in range(n_y):
        first = lax.dot_general(
            x_all, grads[y, :, : 2 * ff], contract_first, preferred_element_type=F32
        )
        second = lax.dot_general(
            g_all, grads[y, :, 2 * ff :], contract_first, preferred_element_type=F32
        )
        weight_grads.append(jnp.concatenate([first.astype(BF16), second.astype(BF16)], axis=1))
    weight_grads = lax.psum_scatter(
        jnp.stack(weight_grads), "expert", scatter_dimension=0, axis_index_groups=along_y
    ).astype(F32)

    input_grad = jnp.zeros((rows, cols), F32)
    for y in range(n_y):
        input_grad = input_grad + lax.dot_general(
            grads[y, :, : 2 * ff],
            weights[y, :, : 2 * ff],
            contract_last,
            preferred_element_type=F32,
        )
    score = score.reshape(n_y, n_z, tok).transpose(1, 2, 0)
    score = jnp.stack(
        [jnp.where(upper_half, 0.0, score), jnp.where(upper_half, score, 0.0)], axis=3
    )
    score = score.reshape(n_z, tok, experts).astype(BF16)
    score = jnp.pad(score, ((0, 0), (0, (n_x - 1) * tok), (0, 128 - experts)))
    back = jnp.concatenate(
        [input_grad.astype(BF16).reshape(n_z, n_x * tok, cols), score], axis=2
    )
    back = back.reshape((q, r) + back.shape[1:]).transpose(1, 0, 2, 3)
    back = jnp.sum(exchange(back, "expert", near_z).astype(F32), axis=0).astype(BF16)
    back = jnp.sum(exchange(back, "expert", far_z).astype(F32), axis=0)
    score = back[:tok, cols : cols + experts]
    grad_combine = jnp.sum(jnp.where(chosen, score[:, None, :], 0.0), axis=2)[None]
    passed = exchange(back[:, :cols].astype(BF16).reshape(n_x, tok, cols), "dp")
    passed = passed.transpose(1, 0, 2).reshape(1, tok, width)
    sections = lax.axis_size("pipe")
    passed = lax.ppermute(passed, "pipe", [(s, (s - 1) % sections) for s in range(sections)])
    return (
        passed,
        grad_combine,
        weight_grads[None, :, :ff],
        weight_grads[None, :, ff : 2 * ff],
        weight_grads[None, :, 2 * ff :],
    )


def solution(mesh):
    row_spec = P("pipe", ("expert", "dp"), None)
    weight_spec = P("pipe", "dp", "expert")
    in_specs = (row_spec,) * 4 + (weight_spec,) * 3
    out_specs = (row_spec,) * 2 + (weight_spec,) * 3
    return jax.shard_map(body, mesh=mesh, in_specs=in_specs, out_specs=out_specs, check_vma=False)
```

```python
import jax
import jax.numpy as jnp
from jax import lax
from jax.sharding import PartitionSpec as P

BF16 = jnp.bfloat16
F32 = jnp.float32
contract_first = (((0,), (0,)), ((), ()))
contract_last = (((1,), (1,)), ((), ()))


def exchange(blocks, axis, groups=None):
    return lax.all_to_all(blocks, axis, 0, 0, axis_index_groups=groups, tiled=True)


def body(tokens, grad_out, routes, combine, w_gate, w_up, w_down):
    tok, width = tokens.shape[1:]
    experts = 8
    n_x = lax.axis_size("dp")
    n_e = lax.axis_size("expert")
    n_z = 2 * (n_e // experts)
    n_y = n_e // n_z
    half = n_z // 2
    quarter = half // 2
    cols = width // n_x
    ff = w_gate.shape[2]
    wide = n_y * ff
    along_y = [[y * n_z + z for y in range(n_y)] for z in range(n_z)]
    same_parity = [[y * n_z + 2 * i + p for i in range(half)] for y in range(n_y) for p in range(2)]
    up_z = [(y * n_z + z, y * n_z + (z + 1) % n_z) for y in range(n_y) for z in range(n_z)]
    down_z = [(b, a) for a, b in up_z]
    upper_half = lax.axis_index("expert") % n_z >= half

    def swap_parity(blocks):
        low = lax.ppermute(blocks[:quarter], "expert", up_z)
        high = lax.ppermute(blocks[quarter:], "expert", down_z)
        return low, high

    weights = jnp.stack([w_gate[0], w_up[0], w_down[0]])
    weights = lax.all_gather(weights, "expert", axis_index_groups=along_y)
    weights = weights.transpose(2, 1, 0, 3).reshape(cols, 3 * wide)

    both = jnp.concatenate([tokens[0], grad_out[0]], axis=0).reshape(2 * tok, n_x, cols)
    both = exchange(both.transpose(1, 0, 2), "dp")
    chosen = routes[0][:, :, None] == jnp.arange(experts, dtype=jnp.int32)
    dense = jnp.sum(jnp.where(chosen, combine[0].astype(F32)[:, :, None], 0.0), axis=1)
    dense = jnp.pad(dense.astype(BF16), ((0, (n_x - 1) * tok), (0, 0)))
    both = jnp.concatenate(
        [
            both[:, :tok].reshape(n_x * tok, cols),
            both[:, tok:].reshape(n_x * tok, cols),
            dense,
        ],
        axis=1,
    )
    own = lax.all_gather(both, "expert", axis_index_groups=same_parity)
    low, high = swap_parity(own)
    low, high, weights = lax.optimization_barrier((low, high, weights))
    rows = jnp.concatenate([own, low, high], axis=0).reshape(n_z, n_x, tok, -1)
    rows = rows.transpose(1, 0, 2, 3)
    route_weight = rows[0]
    rows = rows.reshape(n_x * n_z * tok, -1)
    x_rows = rows[:, :cols]
    g_rows = rows[:, cols : 2 * cols]

    first = jnp.dot(x_rows, weights[:, : 2 * wide], preferred_element_type=F32)
    second = jnp.dot(g_rows, weights[:, 2 * wide :], preferred_element_type=F32)
    partial = jnp.concatenate([first.astype(BF16), second.astype(BF16)], axis=1)
    partial = exchange(partial.reshape(n_x, n_z * tok, 3 * wide), "dp")
    full = jnp.sum(partial.astype(F32), axis=0)

    route_weight = route_weight.reshape(n_z * tok, -1)[:, 2 * cols : 2 * cols + experts]
    route_weight = route_weight.astype(F32).reshape(n_z * tok, n_y, 2)
    route_weight = jnp.where(upper_half, route_weight[:, :, 1], route_weight[:, :, 0])
    route_weight = jnp.broadcast_to(route_weight[:, :, None], (n_z * tok, n_y, ff))
    route_weight = route_weight.reshape(n_z * tok, wide)
    gate = full[:, :wide]
    up = full[:, wide : 2 * wide]
    down_grad = full[:, 2 * wide :]
    sig = jax.nn.sigmoid(gate)
    act = gate * sig
    hidden = act * up
    score = jnp.sum((hidden * down_grad).reshape(n_z, tok, n_y, ff), axis=3)
    score = jnp.stack(
        [jnp.where(upper_half, 0.0, score), jnp.where(upper_half, score, 0.0)], axis=3
    )
    score = score.reshape(n_z, tok, experts).astype(BF16)
    score = jnp.pad(score, ((0, 0), (0, (n_x - 1) * tok), (0, 128 - experts)))
    hidden_grad = down_grad * route_weight
    gate_grad = hidden_grad * up * sig * (1.0 + gate * (1.0 - sig))
    up_grad = hidden_grad * act
    grads = jnp.concatenate(
        [gate_grad.astype(BF16), up_grad.astype(BF16), (hidden * route_weight).astype(BF16)],
        axis=1,
    )
    grads = exchange(jnp.broadcast_to(grads[None], (n_x,) + grads.shape), "dp")
    grads = grads.reshape(n_x * n_z * tok, 3 * wide)

    back = lax.dot_general(
        grads[:, : 2 * wide], weights[:, : 2 * wide], contract_last, preferred_element_type=F32
    )
    back = back.astype(BF16).reshape(n_x, n_z, tok, cols).transpose(1, 0, 2, 3)
    back = jnp.concatenate([back.reshape(n_z, n_x * tok, cols), score], axis=2)
    low, high = swap_parity(back[half:])

    first = lax.dot_general(
        x_rows, grads[:, : 2 * wide], contract_first, preferred_element_type=F32
    )
    second = lax.dot_general(
        g_rows, grads[:, 2 * wide :], contract_first, preferred_element_type=F32
    )
    total = jnp.concatenate([first.astype(BF16), second.astype(BF16)], axis=1)
    total = total.reshape(cols, 3, n_y, ff).transpose(2, 1, 0, 3)
    low, high, total = lax.optimization_barrier((low, high, total))
    total = lax.psum_scatter(total, "expert", scatter_dimension=0, axis_index_groups=along_y)
    total = total.astype(F32)

    back = back[:half].astype(F32) + jnp.concatenate([low, high], axis=0).astype(F32)
    back = exchange(back.astype(BF16), "expert", same_parity)
    back = jnp.sum(back.astype(F32), axis=0)
    score = back[:tok, cols : cols + experts]
    grad_combine = jnp.sum(jnp.where(chosen, score[:, None, :], 0.0), axis=2)[None]
    passed = exchange(back[:, :cols].astype(BF16).reshape(n_x, tok, cols), "dp")
    passed = passed.transpose(1, 0, 2).reshape(1, tok, width)
    sections = lax.axis_size("pipe")
    passed = lax.ppermute(passed, "pipe", [(s, (s - 1) % sections) for s in range(sections)])
    return passed, grad_combine, total[0:1], total[1:2], total[2:3]


def solution(mesh):
    row_spec = P("pipe", ("expert", "dp"), None)
    weight_spec = P("pipe", "dp", "expert")
    in_specs = (row_spec,) * 4 + (weight_spec,) * 3
    out_specs = (row_spec,) * 2 + (weight_spec,) * 3
    return jax.shard_map(body, mesh=mesh, in_specs=in_specs, out_specs=out_specs, check_vma=False)
```

```python
import functools

import jax
import jax.numpy as jnp
from jax import lax
from jax.experimental import pallas as pl
from jax.experimental.pallas import tpu as pltpu
from jax.sharding import PartitionSpec as P

BF16 = jnp.bfloat16
F32 = jnp.float32
LANES = 128
contract_first = (((0,), (0,)), ((), ()))
contract_last = (((1,), (1,)), ((), ()))


def exchange(blocks, axis, groups=None):
    return lax.all_to_all(blocks, axis, 0, 0, axis_index_groups=groups, tiled=True)


def whole(shape):
    return pl.BlockSpec(shape, lambda y: (0,) * len(shape))


def params():
    return pltpu.CompilerParams(
        dimension_semantics=("arbitrary",), vmem_limit_bytes=20 * 1024 * 1024
    )


def gather_rows(n_x, cols, own, low, high, outs):
    count = own.shape[0]
    quarter = low.shape[0]
    for x in range(n_x):
        base = 2 * x * count
        for part, out in enumerate(outs):
            lanes = slice((2 * x + part) * cols, (2 * x + part + 1) * cols)
            out[base : base + count, :] = own[:, lanes]
            out[base + count : base + count + quarter, :] = low[:, lanes]
            out[base + count + quarter : base + 2 * count, :] = high[:, lanes]


def forward_kernel(n_x, cols, own, low, high, weights, partial, x_rows, g_rows, held, arrived):
    y = pl.program_id(0)
    ff = weights.shape[3]

    def copies(step):
        return [
            pltpu.make_async_copy(
                weights.at[step, k],
                held.at[step, :, k * ff : (k + 1) * ff],
                arrived.at[step, k],
            )
            for k in range(3)
        ]

    @pl.when(y == 0)
    def _():
        for step in range(held.shape[0]):
            for copy in copies(step):
                copy.start()
        gather_rows(n_x, cols, own, low, high, (x_rows, g_rows))

    for copy in copies(y):
        copy.wait()
    first = jnp.dot(x_rows[...], held[y, :, : 2 * ff], preferred_element_type=F32)
    partial[:, : 2 * ff] = first.astype(BF16)
    second = jnp.dot(g_rows[...], held[y, :, 2 * ff :], preferred_element_type=F32)
    partial[:, 2 * ff :] = second.astype(BF16)


def forward(own, low, high, weights, n_x):
    n_y, three, cols, ff = weights.shape
    rows = 2 * n_x * own.shape[0]
    return pl.pallas_call(
        functools.partial(forward_kernel, n_x, cols),
        grid=(n_y,),
        in_specs=[
            whole(own.shape),
            whole(low.shape),
            whole(high.shape),
            pl.BlockSpec(memory_space=pltpu.HBM),
        ],
        out_specs=pl.BlockSpec((rows, three * ff), lambda y: (0, y)),
        out_shape=pltpu.HBM((rows, n_y * three * ff), BF16),
        scratch_shapes=[
            pltpu.VMEM((rows, cols), BF16),
            pltpu.VMEM((rows, cols), BF16),
            pltpu.VMEM((n_y, cols, three * ff), BF16),
            pltpu.SemaphoreType.DMA((n_y, three)),
        ],
        compiler_params=params(),
        cost_estimate=pl.CostEstimate(
            flops=2 * rows * cols * n_y * three * ff, bytes_accessed=7_000_000, transcendentals=0
        ),
    )(own, low, high, weights)


def hidden_kernel(half, partial, own, low, high, grads, score):
    n_x, rows, total = partial.shape
    ff = total // 3
    y = pl.program_id(0)
    column = 2 * y + half[0]
    dense = jnp.concatenate([own[...], low[...], high[...]], axis=0).astype(F32)
    lane = lax.broadcasted_iota(jnp.int32, dense.shape, 1)
    route = jnp.sum(jnp.where(lane == column, dense, 0.0), axis=1, keepdims=True)
    full = partial[0].astype(F32)
    for x in range(1, n_x):
        full = full + partial[x].astype(F32)
    gate = full[:, :ff]
    up = full[:, ff : 2 * ff]
    down_grad = full[:, 2 * ff :]
    sig = jax.nn.sigmoid(gate)
    act = gate * sig
    hidden = act * up
    total_score = jnp.sum(hidden * down_grad, axis=1, keepdims=True)
    placed = jnp.where(lane == column, total_score, 0.0).astype(BF16)

    @pl.when(y == 0)
    def _():
        score[...] = placed

    @pl.when(y > 0)
    def _():
        score[...] += placed

    hidden_grad = down_grad * route
    gate_grad = (hidden_grad * up * sig * (1.0 + gate * (1.0 - sig))).astype(BF16)
    up_grad = (hidden_grad * act).astype(BF16)
    weighted = (hidden * route).astype(BF16)
    for x in range(n_x):
        grads[x, :, :ff] = gate_grad
        grads[x, :, ff : 2 * ff] = up_grad
        grads[x, :, 2 * ff :] = weighted


def hidden_part(half, partial, own, low, high, n_y):
    n_x, rows, total = partial.shape
    lanes = own.shape[1] // LANES - 1
    block = pl.BlockSpec((n_x, rows, total // n_y), lambda y: (0, 0, y))
    tails = [pl.BlockSpec((p.shape[0], LANES), lambda y: (0, lanes)) for p in (own, low, high)]
    return pl.pallas_call(
        hidden_kernel,
        grid=(n_y,),
        in_specs=[pl.BlockSpec(memory_space=pltpu.SMEM), block] + tails,
        out_specs=[block, whole((rows, LANES))],
        out_shape=[
            pltpu.HBM(partial.shape, BF16),
            jax.ShapeDtypeStruct((rows, LANES), BF16),
        ],
        compiler_params=params(),
        cost_estimate=pl.CostEstimate(
            flops=20 * rows * total, bytes_accessed=4 * n_x * rows * total, transcendentals=rows * total // 3
        ),
    )(half, partial, own, low, high)


def input_kernel(n_x, grads, weights, score, mine, low, high, total, held, arrived):
    n_y = weights.shape[0]
    ff = weights.shape[3]
    cols = weights.shape[2]
    rows = score.shape[0]
    copies = []
    for y in range(n_y):
        for k in range(2):
            copies.append(
                pltpu.make_async_copy(
                    weights.at[y, k], held.at[y, :, k * ff : (k + 1) * ff], arrived.at[y, k]
                )
            )
    for copy in copies:
        copy.start()
    for y in range(n_y):
        copies[2 * y].wait()
        copies[2 * y + 1].wait()
        product = lax.dot_general(
            grads[:, 3 * y * ff : (3 * y + 2) * ff],
            held[y],
            contract_last,
            preferred_element_type=F32,
        )
        if y == 0:
            total[...] = product
        else:
            total[...] += product
    first = 0
    for out in (mine, low, high):
        count = out.shape[0]
        for x in range(n_x):
            part = total[x * rows + first : x * rows + first + count, :]
            out[:, x * cols : (x + 1) * cols] = part.astype(BF16)
        out[:, n_x * cols :] = score[first : first + count, :]
        first += count


def input_grad(grads, weights, score, n_x):
    n_y, three, cols, ff = weights.shape
    rows = score.shape[0]
    width = n_x * cols + score.shape[1]
    counts = (rows // 2, rows // 4, rows // 4)
    vmem = pl.BlockSpec(memory_space=pltpu.VMEM)
    return pl.pallas_call(
        functools.partial(input_kernel, n_x),
        in_specs=[vmem, pl.BlockSpec(memory_space=pltpu.HBM), vmem],
        out_specs=[vmem] * 3,
        out_shape=[jax.ShapeDtypeStruct((count, width), BF16) for count in counts],
        scratch_shapes=[
            pltpu.VMEM((n_x * rows, cols), F32),
            pltpu.VMEM((n_y, cols, 2 * ff), BF16),
            pltpu.SemaphoreType.DMA((n_y, 2)),
        ],
        compiler_params=pltpu.CompilerParams(vmem_limit_bytes=20 * 1024 * 1024),
        cost_estimate=pl.CostEstimate(
            flops=4 * n_x * rows * cols * n_y * ff, bytes_accessed=6_000_000, transcendentals=0
        ),
    )(grads, weights, score)


def weight_kernel(n_x, cols, own, low, high, grads, out, x_rows, g_rows):
    ff = out.shape[3]

    @pl.when(pl.program_id(0) == 0)
    def _():
        gather_rows(n_x, cols, own, low, high, (x_rows, g_rows))

    product = lax.dot_general(
        x_rows[...], grads[:, : 2 * ff], contract_first, preferred_element_type=F32
    )
    out[0, 0] = product[:, :ff].astype(BF16)
    out[0, 1] = product[:, ff:].astype(BF16)
    product = lax.dot_general(
        g_rows[...], grads[:, 2 * ff :], contract_first, preferred_element_type=F32
    )
    out[0, 2] = product.astype(BF16)


def weight_grad(own, low, high, grads, n_x, n_y, cols):
    rows, total = grads.shape
    ff = total // (3 * n_y)
    return pl.pallas_call(
        functools.partial(weight_kernel, n_x, cols),
        grid=(n_y,),
        in_specs=[
            whole(own.shape),
            whole(low.shape),
            whole(high.shape),
            pl.BlockSpec((rows, 3 * ff), lambda y: (0, y)),
        ],
        out_specs=pl.BlockSpec((1, 3, cols, ff), lambda y: (y, 0, 0, 0)),
        out_shape=pltpu.HBM((n_y, 3, cols, ff), BF16),
        scratch_shapes=[pltpu.VMEM((rows, cols), BF16), pltpu.VMEM((rows, cols), BF16)],
        compiler_params=params(),
        cost_estimate=pl.CostEstimate(
            flops=6 * rows * cols * n_y * ff, bytes_accessed=7_000_000, transcendentals=0
        ),
    )(own, low, high, grads)


def body(tokens, grad_out, routes, combine, w_gate, w_up, w_down):
    tok, width = tokens.shape[1:]
    experts = 8
    n_x = lax.axis_size("dp")
    n_e = lax.axis_size("expert")
    n_z = 2 * (n_e // experts)
    n_y = n_e // n_z
    half = n_z // 2
    cols = width // n_x
    along_y = [[y * n_z + z for y in range(n_y)] for z in range(n_z)]
    same_parity = [[y * n_z + 2 * i + p for i in range(half)] for y in range(n_y) for p in range(2)]
    up_z = [(y * n_z + z, y * n_z + (z + 1) % n_z) for y in range(n_y) for z in range(n_z)]
    down_z = [(b, a) for a, b in up_z]
    upper_half = (lax.axis_index("expert") % n_z >= half).astype(jnp.int32)
    own_rows = half * tok
    all_rows = n_z * tok

    both = jnp.concatenate([tokens[0], grad_out[0]], axis=0).reshape(2 * tok, n_x, cols)
    both = both.transpose(1, 0, 2)
    both, w_gate, w_up, w_down = lax.optimization_barrier((both, w_gate, w_up, w_down))

    weights = jnp.stack([w_gate[0], w_up[0], w_down[0]])
    weights = lax.all_gather(weights, "expert", axis_index_groups=along_y)

    both = exchange(both, "dp")
    chosen = routes[0][:, :, None] == jnp.arange(experts, dtype=jnp.int32)
    dense = jnp.sum(jnp.where(chosen, combine[0].astype(F32)[:, :, None], 0.0), axis=1)
    dense = jnp.pad(dense.astype(BF16), ((0, 0), (0, LANES - experts)))
    pieces = [both[x, p * tok : (p + 1) * tok] for x in range(n_x) for p in range(2)]
    line = jnp.concatenate(pieces + [dense], axis=1)

    own = lax.all_gather(line, "expert", axis_index_groups=same_parity, tiled=True)
    low = lax.ppermute(own[: own_rows // 2], "expert", up_z)
    high = lax.ppermute(own[own_rows // 2 :], "expert", down_z)
    partial = forward(own, low, high, weights, n_x)
    partial = exchange(partial.reshape(n_x, all_rows, -1), "dp")
    grads, score = hidden_part(upper_half[None], partial, own, low, high, n_y)
    grads = exchange(grads, "dp").reshape(n_x * all_rows, -1)

    total = weight_grad(own, low, high, grads, n_x, n_y, cols)
    total, grads = lax.optimization_barrier((total, grads))
    total = lax.psum_scatter(total, "expert", scatter_dimension=0, axis_index_groups=along_y)

    mine, send_up, send_down = input_grad(grads, weights, score, n_x)
    from_below = lax.ppermute(send_up, "expert", up_z)
    from_above = lax.ppermute(send_down, "expert", down_z)
    back = mine.astype(F32) + jnp.concatenate([from_below, from_above], axis=0).astype(F32)
    back = exchange(back.astype(BF16).reshape(half, tok, -1), "expert", same_parity)
    back = jnp.sum(back.astype(F32), axis=0)
    back, total = lax.optimization_barrier((back, total))
    grads = [total[k : k + 1].astype(F32) for k in range(3)]
    score = back[:, width : width + experts]
    grad_combine = jnp.sum(jnp.where(chosen, score[:, None, :], 0.0), axis=2)[None]
    passed = jnp.stack([back[:, x * cols : (x + 1) * cols] for x in range(n_x)])
    passed = exchange(passed.astype(BF16), "dp")
    passed = jnp.concatenate([passed[x] for x in range(n_x)], axis=1)[None]
    passed, grads = lax.optimization_barrier((passed, grads))
    sections = lax.axis_size("pipe")
    passed = lax.ppermute(passed, "pipe", [(s, (s - 1) % sections) for s in range(sections)])
    return passed, grad_combine, *grads


def solution(mesh):
    row_spec = P("pipe", ("expert", "dp"), None)
    weight_spec = P("pipe", "dp", "expert")
    in_specs = (row_spec,) * 4 + (weight_spec,) * 3
    out_specs = (row_spec,) * 2 + (weight_spec,) * 3
    return jax.shard_map(body, mesh=mesh, in_specs=in_specs, out_specs=out_specs, check_vma=False)
```

```python
import functools

import jax
import jax.numpy as jnp
from jax import lax
from jax.experimental import pallas as pl
from jax.experimental.pallas import tpu as pltpu
from jax.sharding import PartitionSpec as P

BF16 = jnp.bfloat16
F32 = jnp.float32
LANES = 128
contract_first = (((0,), (0,)), ((), ()))
contract_last = (((1,), (1,)), ((), ()))


def exchange(blocks, axis, groups=None):
    return lax.all_to_all(blocks, axis, 0, 0, axis_index_groups=groups, tiled=True)


def whole(shape):
    return pl.BlockSpec(shape, lambda y: (0,) * len(shape))


def params():
    return pltpu.CompilerParams(
        dimension_semantics=("arbitrary",), vmem_limit_bytes=20 * 1024 * 1024
    )


def gather_rows(n_x, cols, own, low, high, outs):
    count = own.shape[0]
    quarter = low.shape[0]
    for x in range(n_x):
        base = 2 * x * count
        for part, out in enumerate(outs):
            lanes = slice((2 * x + part) * cols, (2 * x + part + 1) * cols)
            out[base : base + count, :] = own[:, lanes]
            out[base + count : base + count + quarter, :] = low[:, lanes]
            out[base + count + quarter : base + 2 * count, :] = high[:, lanes]


def forward_kernel(n_x, cols, own, low, high, weights, partial, x_rows, g_rows):
    ff = weights.shape[3]

    @pl.when(pl.program_id(0) == 0)
    def _():
        gather_rows(n_x, cols, own, low, high, (x_rows, g_rows))

    pair = jnp.concatenate([weights[0, 0], weights[0, 1]], axis=1)
    first = jnp.dot(x_rows[...], pair, preferred_element_type=F32)
    partial[:, : 2 * ff] = first.astype(BF16)
    second = jnp.dot(g_rows[...], weights[0, 2], preferred_element_type=F32)
    partial[:, 2 * ff :] = second.astype(BF16)


def forward(own, low, high, weights, n_x):
    n_y, three, cols, ff = weights.shape
    rows = 2 * n_x * own.shape[0]
    return pl.pallas_call(
        functools.partial(forward_kernel, n_x, cols),
        grid=(n_y,),
        in_specs=[
            whole(own.shape),
            whole(low.shape),
            whole(high.shape),
            pl.BlockSpec((1, three, cols, ff), lambda y: (y, 0, 0, 0)),
        ],
        out_specs=pl.BlockSpec((rows, three * ff), lambda y: (0, y)),
        out_shape=pltpu.HBM((rows, n_y * three * ff), BF16),
        scratch_shapes=[pltpu.VMEM((rows, cols), BF16), pltpu.VMEM((rows, cols), BF16)],
        compiler_params=params(),
        cost_estimate=pl.CostEstimate(
            flops=2 * rows * cols * n_y * three * ff, bytes_accessed=7_000_000, transcendentals=0
        ),
    )(own, low, high, weights)


def hidden_kernel(half, partial, own, low, high, grads, score):
    n_x, rows, total = partial.shape
    ff = total // 3
    y = pl.program_id(0)
    column = 2 * y + half[0]
    dense = jnp.concatenate([own[...], low[...], high[...]], axis=0).astype(F32)
    lane = lax.broadcasted_iota(jnp.int32, dense.shape, 1)
    route = jnp.sum(jnp.where(lane == column, dense, 0.0), axis=1, keepdims=True)
    full = partial[0].astype(F32)
    for x in range(1, n_x):
        full = full + partial[x].astype(F32)
    gate = full[:, :ff]
    up = full[:, ff : 2 * ff]
    down_grad = full[:, 2 * ff :]
    sig = jax.nn.sigmoid(gate)
    act = gate * sig
    hidden = act * up
    total_score = jnp.sum(hidden * down_grad, axis=1, keepdims=True)
    placed = jnp.where(lane == column, total_score, 0.0).astype(BF16)

    @pl.when(y == 0)
    def _():
        score[...] = placed

    @pl.when(y > 0)
    def _():
        score[...] += placed

    hidden_grad = down_grad * route
    gate_grad = (hidden_grad * up * sig * (1.0 + gate * (1.0 - sig))).astype(BF16)
    up_grad = (hidden_grad * act).astype(BF16)
    weighted = (hidden * route).astype(BF16)
    for x in range(n_x):
        grads[x, :, :ff] = gate_grad
        grads[x, :, ff : 2 * ff] = up_grad
        grads[x, :, 2 * ff :] = weighted


def hidden_part(half, partial, own, low, high, n_y):
    n_x, rows, total = partial.shape
    lanes = own.shape[1] // LANES - 1
    block = pl.BlockSpec((n_x, rows, total // n_y), lambda y: (0, 0, y))
    tails = [pl.BlockSpec((p.shape[0], LANES), lambda y: (0, lanes)) for p in (own, low, high)]
    return pl.pallas_call(
        hidden_kernel,
        grid=(n_y,),
        in_specs=[pl.BlockSpec(memory_space=pltpu.SMEM), block] + tails,
        out_specs=[block, whole((rows, LANES))],
        out_shape=[
            pltpu.HBM(partial.shape, BF16),
            jax.ShapeDtypeStruct((rows, LANES), BF16),
        ],
        compiler_params=params(),
        cost_estimate=pl.CostEstimate(
            flops=20 * rows * total, bytes_accessed=4 * n_x * rows * total, transcendentals=rows * total // 3
        ),
    )(half, partial, own, low, high)


def input_kernel(n_x, grads, weights, score, mine, low, high, total, held, arrived):
    n_y = weights.shape[0]
    ff = weights.shape[3]
    cols = weights.shape[2]
    rows = score.shape[0]
    copies = []
    for y in range(n_y):
        for k in range(2):
            copies.append(
                pltpu.make_async_copy(
                    weights.at[y, k], held.at[y, :, k * ff : (k + 1) * ff], arrived.at[y, k]
                )
            )
    for copy in copies:
        copy.start()
    for y in range(n_y):
        copies[2 * y].wait()
        copies[2 * y + 1].wait()
        product = lax.dot_general(
            grads[:, 3 * y * ff : (3 * y + 2) * ff],
            held[y],
            contract_last,
            preferred_element_type=F32,
        )
        if y == 0:
            total[...] = product
        else:
            total[...] += product
    first = 0
    for out in (mine, low, high):
        count = out.shape[0]
        for x in range(n_x):
            part = total[x * rows + first : x * rows + first + count, :]
            out[:, x * cols : (x + 1) * cols] = part.astype(BF16)
        out[:, n_x * cols :] = score[first : first + count, :]
        first += count


def input_grad(grads, weights, score, n_x):
    n_y, three, cols, ff = weights.shape
    rows = score.shape[0]
    width = n_x * cols + score.shape[1]
    counts = (rows // 2, rows // 4, rows // 4)
    vmem = pl.BlockSpec(memory_space=pltpu.VMEM)
    return pl.pallas_call(
        functools.partial(input_kernel, n_x),
        in_specs=[vmem, pl.BlockSpec(memory_space=pltpu.HBM), vmem],
        out_specs=[vmem] * 3,
        out_shape=[jax.ShapeDtypeStruct((count, width), BF16) for count in counts],
        scratch_shapes=[
            pltpu.VMEM((n_x * rows, cols), F32),
            pltpu.VMEM((n_y, cols, 2 * ff), BF16),
            pltpu.SemaphoreType.DMA((n_y, 2)),
        ],
        compiler_params=pltpu.CompilerParams(vmem_limit_bytes=20 * 1024 * 1024),
        cost_estimate=pl.CostEstimate(
            flops=4 * n_x * rows * cols * n_y * ff, bytes_accessed=6_000_000, transcendentals=0
        ),
    )(grads, weights, score)


def weight_kernel(n_x, cols, own, low, high, grads, out, x_rows, g_rows):
    ff = out.shape[3]

    @pl.when(pl.program_id(0) == 0)
    def _():
        gather_rows(n_x, cols, own, low, high, (x_rows, g_rows))

    product = lax.dot_general(
        x_rows[...], grads[:, : 2 * ff], contract_first, preferred_element_type=F32
    )
    out[0, 0] = product[:, :ff].astype(BF16)
    out[0, 1] = product[:, ff:].astype(BF16)
    product = lax.dot_general(
        g_rows[...], grads[:, 2 * ff :], contract_first, preferred_element_type=F32
    )
    out[0, 2] = product.astype(BF16)


def weight_grad(own, low, high, grads, n_x, n_y, cols):
    rows, total = grads.shape
    ff = total // (3 * n_y)
    return pl.pallas_call(
        functools.partial(weight_kernel, n_x, cols),
        grid=(n_y,),
        in_specs=[
            whole(own.shape),
            whole(low.shape),
            whole(high.shape),
            pl.BlockSpec((rows, 3 * ff), lambda y: (0, y)),
        ],
        out_specs=pl.BlockSpec((1, 3, cols, ff), lambda y: (y, 0, 0, 0)),
        out_shape=pltpu.HBM((n_y, 3, cols, ff), BF16),
        scratch_shapes=[pltpu.VMEM((rows, cols), BF16), pltpu.VMEM((rows, cols), BF16)],
        compiler_params=params(),
        cost_estimate=pl.CostEstimate(
            flops=6 * rows * cols * n_y * ff, bytes_accessed=7_000_000, transcendentals=0
        ),
    )(own, low, high, grads)


def body(tokens, grad_out, routes, combine, w_gate, w_up, w_down):
    tok, width = tokens.shape[1:]
    experts = 8
    n_x = lax.axis_size("dp")
    n_e = lax.axis_size("expert")
    n_z = 2 * (n_e // experts)
    n_y = n_e // n_z
    half = n_z // 2
    cols = width // n_x
    along_y = [[y * n_z + z for y in range(n_y)] for z in range(n_z)]
    same_parity = [[y * n_z + 2 * i + p for i in range(half)] for y in range(n_y) for p in range(2)]
    up_z = [(y * n_z + z, y * n_z + (z + 1) % n_z) for y in range(n_y) for z in range(n_z)]
    down_z = [(b, a) for a, b in up_z]
    upper_half = (lax.axis_index("expert") % n_z >= half).astype(jnp.int32)
    own_rows = half * tok
    all_rows = n_z * tok

    both = jnp.concatenate([tokens[0], grad_out[0]], axis=0).reshape(2 * tok, n_x, cols)
    both = both.transpose(1, 0, 2)
    both, w_gate, w_up, w_down = lax.optimization_barrier((both, w_gate, w_up, w_down))

    weights = jnp.stack([w_gate[0], w_up[0], w_down[0]])
    weights = lax.all_gather(weights, "expert", axis_index_groups=along_y)

    both = exchange(both, "dp")
    chosen = routes[0][:, :, None] == jnp.arange(experts, dtype=jnp.int32)
    dense = jnp.sum(jnp.where(chosen, combine[0].astype(F32)[:, :, None], 0.0), axis=1)
    dense = jnp.pad(dense.astype(BF16), ((0, 0), (0, LANES - experts)))
    pieces = [both[x, p * tok : (p + 1) * tok] for x in range(n_x) for p in range(2)]
    line = jnp.concatenate(pieces + [dense], axis=1)

    own = lax.all_gather(line, "expert", axis_index_groups=same_parity, tiled=True)
    low = lax.ppermute(own[: own_rows // 2], "expert", up_z)
    high = lax.ppermute(own[own_rows // 2 :], "expert", down_z)
    partial = forward(own, low, high, weights, n_x)
    partial = exchange(partial.reshape(n_x, all_rows, -1), "dp")
    grads, score = hidden_part(upper_half[None], partial, own, low, high, n_y)
    grads = exchange(grads, "dp").reshape(n_x * all_rows, -1)

    mine, send_up, send_down = input_grad(grads, weights, score, n_x)
    send_up, send_down, grads = lax.optimization_barrier((send_up, send_down, grads))
    from_below = lax.ppermute(send_up, "expert", up_z)
    from_above = lax.ppermute(send_down, "expert", down_z)

    total = weight_grad(own, low, high, grads, n_x, n_y, cols)
    from_below, from_above, _ = lax.optimization_barrier((from_below, from_above, total))
    total = lax.psum_scatter(total, "expert", scatter_dimension=0, axis_index_groups=along_y)

    back = mine.astype(F32) + jnp.concatenate([from_below, from_above], axis=0).astype(F32)
    back = exchange(back.astype(BF16).reshape(half, tok, -1), "expert", same_parity)
    back = jnp.sum(back.astype(F32), axis=0)
    score = back[:, width : width + experts]
    grad_combine = jnp.sum(jnp.where(chosen, score[:, None, :], 0.0), axis=2)[None]
    back, grad_combine, total = lax.optimization_barrier((back, grad_combine, total))
    grads = [total[k : k + 1].astype(F32) for k in range(3)]
    passed = jnp.stack([back[:, x * cols : (x + 1) * cols] for x in range(n_x)])
    sections = lax.axis_size("pipe")
    passed = jnp.broadcast_to(passed.astype(BF16)[None], (sections,) + passed.shape)
    passed = exchange(passed.reshape(sections * n_x, tok, cols), ("pipe", "dp"))
    passed, grads = lax.optimization_barrier((passed, grads))
    source = (lax.axis_index("pipe") + 1) % sections
    passed = lax.dynamic_slice_in_dim(passed, source * n_x, n_x, 0)
    passed = jnp.concatenate([passed[x] for x in range(n_x)], axis=1)[None]
    return passed, grad_combine, *grads


def solution(mesh):
    row_spec = P("pipe", ("expert", "dp"), None)
    weight_spec = P("pipe", "dp", "expert")
    in_specs = (row_spec,) * 4 + (weight_spec,) * 3
    out_specs = (row_spec,) * 2 + (weight_spec,) * 3
    return jax.shard_map(body, mesh=mesh, in_specs=in_specs, out_specs=out_specs, check_vma=False)
```

```python
import functools

import jax
import jax.numpy as jnp
from jax import lax
from jax.experimental import pallas as pl
from jax.experimental.pallas import tpu as pltpu
from jax.sharding import PartitionSpec as P

BF16 = jnp.bfloat16
F32 = jnp.float32
LANES = 128
contract_first = (((0,), (0,)), ((), ()))
contract_last = (((1,), (1,)), ((), ()))


def exchange(blocks, axis, groups=None):
    return lax.all_to_all(blocks, axis, 0, 0, axis_index_groups=groups, tiled=True)


def whole(shape):
    return pl.BlockSpec(shape, lambda y: (0,) * len(shape))


def params():
    return pltpu.CompilerParams(
        dimension_semantics=("arbitrary",), vmem_limit_bytes=20 * 1024 * 1024
    )


def gather_rows(n_x, cols, own, low, high, outs):
    count = own.shape[0]
    quarter = low.shape[0]
    for x in range(n_x):
        base = 2 * x * count
        for part, out in enumerate(outs):
            lanes = slice((2 * x + part) * cols, (2 * x + part + 1) * cols)
            out[base : base + count, :] = own[:, lanes]
            out[base + count : base + count + quarter, :] = low[:, lanes]
            out[base + count + quarter : base + 2 * count, :] = high[:, lanes]


def forward_kernel(n_x, cols, own, low, high, weights, partial, x_rows, g_rows):
    ff = weights.shape[3]

    @pl.when(pl.program_id(0) == 0)
    def _():
        gather_rows(n_x, cols, own, low, high, (x_rows, g_rows))

    pair = jnp.concatenate([weights[0, 0], weights[0, 1]], axis=1)
    first = jnp.dot(x_rows[...], pair, preferred_element_type=F32)
    partial[:, : 2 * ff] = first.astype(BF16)
    second = jnp.dot(g_rows[...], weights[0, 2], preferred_element_type=F32)
    partial[:, 2 * ff :] = second.astype(BF16)


def forward(own, low, high, weights, n_x):
    n_y, three, cols, ff = weights.shape
    rows = 2 * n_x * own.shape[0]
    return pl.pallas_call(
        functools.partial(forward_kernel, n_x, cols),
        grid=(n_y,),
        in_specs=[
            whole(own.shape),
            whole(low.shape),
            whole(high.shape),
            pl.BlockSpec((1, three, cols, ff), lambda y: (y, 0, 0, 0)),
        ],
        out_specs=pl.BlockSpec((rows, three * ff), lambda y: (0, y)),
        out_shape=pltpu.HBM((rows, n_y * three * ff), BF16),
        scratch_shapes=[pltpu.VMEM((rows, cols), BF16), pltpu.VMEM((rows, cols), BF16)],
        compiler_params=params(),
        cost_estimate=pl.CostEstimate(
            flops=2 * rows * cols * n_y * three * ff, bytes_accessed=7_000_000, transcendentals=0
        ),
    )(own, low, high, weights)


def hidden_kernel(half, partial, own, low, high, grads, score):
    n_x, rows, total = partial.shape
    ff = total // 3
    y = pl.program_id(0)
    column = 2 * y + half[0]
    dense = jnp.concatenate([own[...], low[...], high[...]], axis=0).astype(F32)
    lane = lax.broadcasted_iota(jnp.int32, dense.shape, 1)
    route = jnp.sum(jnp.where(lane == column, dense, 0.0), axis=1, keepdims=True)
    full = partial[0].astype(F32)
    for x in range(1, n_x):
        full = full + partial[x].astype(F32)
    gate = full[:, :ff]
    up = full[:, ff : 2 * ff]
    down_grad = full[:, 2 * ff :]
    sig = jax.nn.sigmoid(gate)
    act = gate * sig
    hidden = act * up
    total_score = jnp.sum(hidden * down_grad, axis=1, keepdims=True)
    placed = jnp.where(lane == column, total_score, 0.0).astype(BF16)

    @pl.when(y == 0)
    def _():
        score[...] = placed

    @pl.when(y > 0)
    def _():
        score[...] += placed

    hidden_grad = down_grad * route
    gate_grad = (hidden_grad * up * sig * (1.0 + gate * (1.0 - sig))).astype(BF16)
    up_grad = (hidden_grad * act).astype(BF16)
    weighted = (hidden * route).astype(BF16)
    for x in range(n_x):
        grads[x, :, :ff] = gate_grad
        grads[x, :, ff : 2 * ff] = up_grad
        grads[x, :, 2 * ff :] = weighted


def hidden_part(half, partial, own, low, high, n_y):
    n_x, rows, total = partial.shape
    lanes = own.shape[1] // LANES - 1
    block = pl.BlockSpec((n_x, rows, total // n_y), lambda y: (0, 0, y))
    tails = [pl.BlockSpec((p.shape[0], LANES), lambda y: (0, lanes)) for p in (own, low, high)]
    return pl.pallas_call(
        hidden_kernel,
        grid=(n_y,),
        in_specs=[pl.BlockSpec(memory_space=pltpu.SMEM), block] + tails,
        out_specs=[block, whole((rows, LANES))],
        out_shape=[
            jax.ShapeDtypeStruct(partial.shape, BF16),
            jax.ShapeDtypeStruct((rows, LANES), BF16),
        ],
        compiler_params=params(),
        cost_estimate=pl.CostEstimate(
            flops=20 * rows * total, bytes_accessed=4 * n_x * rows * total, transcendentals=rows * total // 3
        ),
    )(half, partial, own, low, high)


def input_kernel(n_x, grads, weights, score, mine, low, high, total, held, arrived):
    n_y = weights.shape[0]
    ff = weights.shape[3]
    cols = weights.shape[2]
    rows = score.shape[0]
    copies = []
    for y in range(n_y):
        for k in range(2):
            copies.append(
                pltpu.make_async_copy(
                    weights.at[y, k], held.at[y, :, k * ff : (k + 1) * ff], arrived.at[y, k]
                )
            )
    for copy in copies:
        copy.start()
    for y in range(n_y):
        copies[2 * y].wait()
        copies[2 * y + 1].wait()
        product = lax.dot_general(
            grads[:, 3 * y * ff : (3 * y + 2) * ff],
            held[y],
            contract_last,
            preferred_element_type=F32,
        )
        if y == 0:
            total[...] = product
        else:
            total[...] += product
    first = 0
    for out in (mine, low, high):
        count = out.shape[0]
        for x in range(n_x):
            part = total[x * rows + first : x * rows + first + count, :]
            out[:, x * cols : (x + 1) * cols] = part.astype(BF16)
        out[:, n_x * cols :] = score[first : first + count, :]
        first += count


def input_grad(grads, weights, score, n_x):
    n_y, three, cols, ff = weights.shape
    rows = score.shape[0]
    width = n_x * cols + score.shape[1]
    counts = (rows // 2, rows // 4, rows // 4)
    vmem = pl.BlockSpec(memory_space=pltpu.VMEM)
    return pl.pallas_call(
        functools.partial(input_kernel, n_x),
        in_specs=[vmem, pl.BlockSpec(memory_space=pltpu.HBM), vmem],
        out_specs=[vmem] * 3,
        out_shape=[jax.ShapeDtypeStruct((count, width), BF16) for count in counts],
        scratch_shapes=[
            pltpu.VMEM((n_x * rows, cols), F32),
            pltpu.VMEM((n_y, cols, 2 * ff), BF16),
            pltpu.SemaphoreType.DMA((n_y, 2)),
        ],
        compiler_params=pltpu.CompilerParams(vmem_limit_bytes=20 * 1024 * 1024),
        cost_estimate=pl.CostEstimate(
            flops=4 * n_x * rows * cols * n_y * ff, bytes_accessed=6_000_000, transcendentals=0
        ),
    )(grads, weights, score)


def weight_kernel(n_x, cols, own, low, high, grads, out, x_rows, g_rows):
    ff = out.shape[3]

    @pl.when(pl.program_id(0) == 0)
    def _():
        gather_rows(n_x, cols, own, low, high, (x_rows, g_rows))

    product = lax.dot_general(
        x_rows[...], grads[:, : 2 * ff], contract_first, preferred_element_type=F32
    )
    out[0, 0] = product[:, :ff].astype(BF16)
    out[0, 1] = product[:, ff:].astype(BF16)
    product = lax.dot_general(
        g_rows[...], grads[:, 2 * ff :], contract_first, preferred_element_type=F32
    )
    out[0, 2] = product.astype(BF16)


def weight_grad(own, low, high, grads, n_x, n_y, cols):
    rows, total = grads.shape
    ff = total // (3 * n_y)
    return pl.pallas_call(
        functools.partial(weight_kernel, n_x, cols),
        grid=(n_y,),
        in_specs=[
            whole(own.shape),
            whole(low.shape),
            whole(high.shape),
            pl.BlockSpec((rows, 3 * ff), lambda y: (0, y)),
        ],
        out_specs=pl.BlockSpec((1, 3, cols, ff), lambda y: (y, 0, 0, 0)),
        out_shape=pltpu.HBM((n_y, 3, cols, ff), BF16),
        scratch_shapes=[pltpu.VMEM((rows, cols), BF16), pltpu.VMEM((rows, cols), BF16)],
        compiler_params=params(),
        cost_estimate=pl.CostEstimate(
            flops=6 * rows * cols * n_y * ff, bytes_accessed=7_000_000, transcendentals=0
        ),
    )(own, low, high, grads)


def body(tokens, grad_out, routes, combine, w_gate, w_up, w_down):
    tok, width = tokens.shape[1:]
    experts = 8
    n_x = lax.axis_size("dp")
    n_e = lax.axis_size("expert")
    n_z = 2 * (n_e // experts)
    n_y = n_e // n_z
    half = n_z // 2
    cols = width // n_x
    along_y = [[y * n_z + z for y in range(n_y)] for z in range(n_z)]
    same_parity = [[y * n_z + 2 * i + p for i in range(half)] for y in range(n_y) for p in range(2)]
    up_z = [(y * n_z + z, y * n_z + (z + 1) % n_z) for y in range(n_y) for z in range(n_z)]
    down_z = [(b, a) for a, b in up_z]
    upper_half = (lax.axis_index("expert") % n_z >= half).astype(jnp.int32)
    own_rows = half * tok
    all_rows = n_z * tok

    both = jnp.concatenate([tokens[0], grad_out[0]], axis=0).reshape(2 * tok, n_x, cols)
    both = both.transpose(1, 0, 2)
    both, w_gate, w_up, w_down = lax.optimization_barrier((both, w_gate, w_up, w_down))

    weights = jnp.stack([w_gate[0], w_up[0], w_down[0]])
    weights = lax.all_gather(weights, "expert", axis_index_groups=along_y)

    both = exchange(both, "dp")
    chosen = routes[0][:, :, None] == jnp.arange(experts, dtype=jnp.int32)
    dense = jnp.sum(jnp.where(chosen, combine[0].astype(F32)[:, :, None], 0.0), axis=1)
    dense = jnp.pad(dense.astype(BF16), ((0, 0), (0, LANES - experts)))
    pieces = [both[x, p * tok : (p + 1) * tok] for x in range(n_x) for p in range(2)]
    line = jnp.concatenate(pieces + [dense], axis=1)

    own = lax.all_gather(line, "expert", axis_index_groups=same_parity, tiled=True)
    low = lax.ppermute(own[: own_rows // 2], "expert", up_z)
    high = lax.ppermute(own[own_rows // 2 :], "expert", down_z)
    partial = forward(own, low, high, weights, n_x)
    partial = exchange(partial.reshape(n_x, all_rows, -1), "dp")
    grads, score = hidden_part(upper_half[None], partial, own, low, high, n_y)
    grads = exchange(grads, "dp").reshape(n_x * all_rows, -1)

    mine, send_up, send_down = input_grad(grads, weights, score, n_x)
    send_up, send_down, grads = lax.optimization_barrier((send_up, send_down, grads))
    from_below = lax.ppermute(send_up, "expert", up_z)
    from_above = lax.ppermute(send_down, "expert", down_z)

    total = weight_grad(own, low, high, grads, n_x, n_y, cols)
    from_below, from_above, _ = lax.optimization_barrier((from_below, from_above, total))
    total = lax.psum_scatter(total, "expert", scatter_dimension=0, axis_index_groups=along_y)

    back = mine.astype(F32) + jnp.concatenate([from_below, from_above], axis=0).astype(F32)
    back = exchange(back.astype(BF16).reshape(half, tok, -1), "expert", same_parity)
    back = jnp.sum(back.astype(F32), axis=0)
    score = back[:, width : width + experts]
    grad_combine = jnp.sum(jnp.where(chosen, score[:, None, :], 0.0), axis=2)[None]
    back, grad_combine, total = lax.optimization_barrier((back, grad_combine, total))
    grads = [total[k : k + 1].astype(F32) for k in range(3)]
    passed = jnp.stack([back[:, x * cols : (x + 1) * cols] for x in range(n_x)])
    sections = lax.axis_size("pipe")
    passed = jnp.broadcast_to(passed.astype(BF16)[None], (sections,) + passed.shape)
    passed = exchange(passed.reshape(sections * n_x, tok, cols), ("pipe", "dp"))
    passed, grads = lax.optimization_barrier((passed, grads))
    source = (lax.axis_index("pipe") + 1) % sections
    passed = lax.dynamic_slice_in_dim(passed, source * n_x, n_x, 0)
    passed = jnp.concatenate([passed[x] for x in range(n_x)], axis=1)[None]
    return passed, grad_combine, *grads


def solution(mesh):
    row_spec = P("pipe", ("expert", "dp"), None)
    weight_spec = P("pipe", "dp", "expert")
    in_specs = (row_spec,) * 4 + (weight_spec,) * 3
    out_specs = (row_spec,) * 2 + (weight_spec,) * 3
    return jax.shard_map(body, mesh=mesh, in_specs=in_specs, out_specs=out_specs, check_vma=False)
```

```python
import functools

import jax
import jax.numpy as jnp
from jax import lax
from jax.experimental import pallas as pl
from jax.experimental.pallas import tpu as pltpu
from jax.sharding import PartitionSpec as P

BF16 = jnp.bfloat16
F32 = jnp.float32
LANES = 128
contract_first = (((0,), (0,)), ((), ()))
contract_last = (((1,), (1,)), ((), ()))


def exchange(blocks, axis, groups=None):
    return lax.all_to_all(blocks, axis, 0, 0, axis_index_groups=groups, tiled=True)


def whole(shape):
    return pl.BlockSpec(shape, lambda y: (0,) * len(shape))


def params():
    return pltpu.CompilerParams(
        dimension_semantics=("arbitrary",), vmem_limit_bytes=12 * 1024 * 1024
    )


def gather_rows(n_x, cols, own, low, high, outs):
    count = own.shape[0]
    quarter = low.shape[0]
    for x in range(n_x):
        base = 2 * x * count
        for part, out in enumerate(outs):
            lanes = slice((2 * x + part) * cols, (2 * x + part + 1) * cols)
            out[base : base + count, :] = own[:, lanes]
            out[base + count : base + count + quarter, :] = low[:, lanes]
            out[base + count + quarter : base + 2 * count, :] = high[:, lanes]


def forward_kernel(n_x, cols, own, low, high, weights, partial, x_rows, g_rows):
    ff = weights.shape[3]

    @pl.when(pl.program_id(0) == 0)
    def _():
        gather_rows(n_x, cols, own, low, high, (x_rows, g_rows))

    pair = jnp.concatenate([weights[0, 0], weights[0, 1]], axis=1)
    first = jnp.dot(x_rows[...], pair, preferred_element_type=F32)
    partial[:, : 2 * ff] = first.astype(BF16)
    second = jnp.dot(g_rows[...], weights[0, 2], preferred_element_type=F32)
    partial[:, 2 * ff :] = second.astype(BF16)


def forward(own, low, high, weights, n_x):
    n_y, three, cols, ff = weights.shape
    rows = 2 * n_x * own.shape[0]
    return pl.pallas_call(
        functools.partial(forward_kernel, n_x, cols),
        grid=(n_y,),
        in_specs=[
            whole(own.shape),
            whole(low.shape),
            whole(high.shape),
            pl.BlockSpec((1, three, cols, ff), lambda y: (y, 0, 0, 0)),
        ],
        out_specs=pl.BlockSpec((rows, three * ff), lambda y: (0, y)),
        out_shape=pltpu.HBM((rows, n_y * three * ff), BF16),
        scratch_shapes=[pltpu.VMEM((rows, cols), BF16), pltpu.VMEM((rows, cols), BF16)],
        compiler_params=params(),
        cost_estimate=pl.CostEstimate(
            flops=2 * rows * cols * n_y * three * ff, bytes_accessed=7_000_000, transcendentals=0
        ),
    )(own, low, high, weights)


def hidden_kernel(half, partial, own, low, high, grads, score):
    n_x, rows, total = partial.shape
    ff = total // 3
    y = pl.program_id(0)
    column = 2 * y + half[0]
    dense = jnp.concatenate([own[...], low[...], high[...]], axis=0).astype(F32)
    lane = lax.broadcasted_iota(jnp.int32, dense.shape, 1)
    route = jnp.sum(jnp.where(lane == column, dense, 0.0), axis=1, keepdims=True)
    full = partial[0].astype(F32)
    for x in range(1, n_x):
        full = full + partial[x].astype(F32)
    gate = full[:, :ff]
    up = full[:, ff : 2 * ff]
    down_grad = full[:, 2 * ff :]
    sig = jax.nn.sigmoid(gate)
    act = gate * sig
    hidden = act * up
    total_score = jnp.sum(hidden * down_grad, axis=1, keepdims=True)
    placed = jnp.where(lane == column, total_score, 0.0).astype(BF16)

    @pl.when(y == 0)
    def _():
        score[...] = placed

    @pl.when(y > 0)
    def _():
        score[...] += placed

    hidden_grad = down_grad * route
    gate_grad = (hidden_grad * up * sig * (1.0 + gate * (1.0 - sig))).astype(BF16)
    up_grad = (hidden_grad * act).astype(BF16)
    weighted = (hidden * route).astype(BF16)
    for x in range(n_x):
        grads[x, :, :ff] = gate_grad
        grads[x, :, ff : 2 * ff] = up_grad
        grads[x, :, 2 * ff :] = weighted


def hidden_part(half, partial, own, low, high, n_y):
    n_x, rows, total = partial.shape
    lanes = own.shape[1] // LANES - 1
    block = pl.BlockSpec((n_x, rows, total // n_y), lambda y: (0, 0, y))
    tails = [pl.BlockSpec((p.shape[0], LANES), lambda y: (0, lanes)) for p in (own, low, high)]
    return pl.pallas_call(
        hidden_kernel,
        grid=(n_y,),
        in_specs=[pl.BlockSpec(memory_space=pltpu.SMEM), block] + tails,
        out_specs=[block, whole((rows, LANES))],
        out_shape=[
            jax.ShapeDtypeStruct(partial.shape, BF16),
            jax.ShapeDtypeStruct((rows, LANES), BF16),
        ],
        compiler_params=params(),
        cost_estimate=pl.CostEstimate(
            flops=20 * rows * total, bytes_accessed=4 * n_x * rows * total, transcendentals=rows * total // 3
        ),
    )(half, partial, own, low, high)


def input_kernel(n_x, grads, weights, score, mine, low, high, total, held, arrived):
    n_y = weights.shape[0]
    ff = weights.shape[3]
    cols = weights.shape[2]
    rows = score.shape[0]
    copies = []
    for y in range(n_y):
        for k in range(2):
            copies.append(
                pltpu.make_async_copy(
                    weights.at[y, k], held.at[y, :, k * ff : (k + 1) * ff], arrived.at[y, k]
                )
            )
    for copy in copies:
        copy.start()
    for y in range(n_y):
        copies[2 * y].wait()
        copies[2 * y + 1].wait()
        product = lax.dot_general(
            grads[:, 3 * y * ff : (3 * y + 2) * ff],
            held[y],
            contract_last,
            preferred_element_type=F32,
        )
        if y == 0:
            total[...] = product
        else:
            total[...] += product
    first = 0
    for out in (mine, low, high):
        count = out.shape[0]
        for x in range(n_x):
            part = total[x * rows + first : x * rows + first + count, :]
            out[:, x * cols : (x + 1) * cols] = part.astype(BF16)
        out[:, n_x * cols :] = score[first : first + count, :]
        first += count


def input_grad(grads, weights, score, n_x):
    n_y, three, cols, ff = weights.shape
    rows = score.shape[0]
    width = n_x * cols + score.shape[1]
    counts = (rows // 2, rows // 4, rows // 4)
    vmem = pl.BlockSpec(memory_space=pltpu.VMEM)
    return pl.pallas_call(
        functools.partial(input_kernel, n_x),
        in_specs=[vmem, pl.BlockSpec(memory_space=pltpu.HBM), vmem],
        out_specs=[vmem] * 3,
        out_shape=[jax.ShapeDtypeStruct((count, width), BF16) for count in counts],
        scratch_shapes=[
            pltpu.VMEM((n_x * rows, cols), F32),
            pltpu.VMEM((n_y, cols, 2 * ff), BF16),
            pltpu.SemaphoreType.DMA((n_y, 2)),
        ],
        compiler_params=pltpu.CompilerParams(vmem_limit_bytes=12 * 1024 * 1024),
        cost_estimate=pl.CostEstimate(
            flops=4 * n_x * rows * cols * n_y * ff, bytes_accessed=6_000_000, transcendentals=0
        ),
    )(grads, weights, score)


def weight_kernel(n_x, cols, own, low, high, grads, out, x_rows, g_rows):
    ff = out.shape[3]

    @pl.when(pl.program_id(0) == 0)
    def _():
        gather_rows(n_x, cols, own, low, high, (x_rows, g_rows))

    product = lax.dot_general(
        x_rows[...], grads[:, : 2 * ff], contract_first, preferred_element_type=F32
    )
    out[0, 0] = product[:, :ff].astype(BF16)
    out[0, 1] = product[:, ff:].astype(BF16)
    product = lax.dot_general(
        g_rows[...], grads[:, 2 * ff :], contract_first, preferred_element_type=F32
    )
    out[0, 2] = product.astype(BF16)


def weight_grad(own, low, high, grads, n_x, n_y, cols):
    rows, total = grads.shape
    ff = total // (3 * n_y)
    return pl.pallas_call(
        functools.partial(weight_kernel, n_x, cols),
        grid=(n_y,),
        in_specs=[
            whole(own.shape),
            whole(low.shape),
            whole(high.shape),
            pl.BlockSpec((rows, 3 * ff), lambda y: (0, y)),
        ],
        out_specs=pl.BlockSpec((1, 3, cols, ff), lambda y: (y, 0, 0, 0)),
        out_shape=pltpu.HBM((n_y, 3, cols, ff), BF16),
        scratch_shapes=[pltpu.VMEM((rows, cols), BF16), pltpu.VMEM((rows, cols), BF16)],
        compiler_params=params(),
        cost_estimate=pl.CostEstimate(
            flops=6 * rows * cols * n_y * ff, bytes_accessed=7_000_000, transcendentals=0
        ),
    )(own, low, high, grads)


def body(tokens, grad_out, routes, combine, w_gate, w_up, w_down):
    tok, width = tokens.shape[1:]
    experts = 8
    n_x = lax.axis_size("dp")
    n_e = lax.axis_size("expert")
    n_z = 2 * (n_e // experts)
    n_y = n_e // n_z
    half = n_z // 2
    cols = width // n_x
    along_y = [[y * n_z + z for y in range(n_y)] for z in range(n_z)]
    same_parity = [[y * n_z + 2 * i + p for i in range(half)] for y in range(n_y) for p in range(2)]
    up_z = [(y * n_z + z, y * n_z + (z + 1) % n_z) for y in range(n_y) for z in range(n_z)]
    down_z = [(b, a) for a, b in up_z]
    upper_half = (lax.axis_index("expert") % n_z >= half).astype(jnp.int32)
    own_rows = half * tok
    all_rows = n_z * tok

    both = jnp.concatenate([tokens[0], grad_out[0]], axis=0).reshape(2 * tok, n_x, cols)
    both = both.transpose(1, 0, 2)
    both, w_gate, w_up, w_down = lax.optimization_barrier((both, w_gate, w_up, w_down))

    weights = jnp.stack([w_gate[0], w_up[0], w_down[0]])
    weights = lax.all_gather(weights, "expert", axis_index_groups=along_y)

    both = exchange(both, "dp")
    chosen = routes[0][:, :, None] == jnp.arange(experts, dtype=jnp.int32)
    dense = jnp.sum(jnp.where(chosen, combine[0].astype(F32)[:, :, None], 0.0), axis=1)
    dense = jnp.pad(dense.astype(BF16), ((0, 0), (0, LANES - experts)))
    pieces = [both[x, p * tok : (p + 1) * tok] for x in range(n_x) for p in range(2)]
    line = jnp.concatenate(pieces + [dense], axis=1)

    own = lax.all_gather(line, "expert", axis_index_groups=same_parity, tiled=True)
    low = lax.ppermute(own[: own_rows // 2], "expert", up_z)
    high = lax.ppermute(own[own_rows // 2 :], "expert", down_z)
    partial = forward(own, low, high, weights, n_x)
    partial = exchange(partial.reshape(n_x, all_rows, -1), "dp")
    grads, score = hidden_part(upper_half[None], partial, own, low, high, n_y)
    grads = exchange(grads, "dp").reshape(n_x * all_rows, -1)

    mine, send_up, send_down = input_grad(grads, weights, score, n_x)
    send_up, send_down, grads = lax.optimization_barrier((send_up, send_down, grads))
    from_below = lax.ppermute(send_up, "expert", up_z)
    from_above = lax.ppermute(send_down, "expert", down_z)

    total = weight_grad(own, low, high, grads, n_x, n_y, cols)
    from_below, from_above, _ = lax.optimization_barrier((from_below, from_above, total))
    total = lax.psum_scatter(total, "expert", scatter_dimension=0, axis_index_groups=along_y)

    back = mine.astype(F32) + jnp.concatenate([from_below, from_above], axis=0).astype(F32)
    back = exchange(back.astype(BF16).reshape(half, tok, -1), "expert", same_parity)
    back = jnp.sum(back.astype(F32), axis=0)
    score = back[:, width : width + experts]
    grad_combine = jnp.sum(jnp.where(chosen, score[:, None, :], 0.0), axis=2)[None]
    back, grad_combine, total = lax.optimization_barrier((back, grad_combine, total))
    grads = [total[k : k + 1].astype(F32) for k in range(3)]
    passed = jnp.stack([back[:, x * cols : (x + 1) * cols] for x in range(n_x)])
    sections = lax.axis_size("pipe")
    passed = jnp.broadcast_to(passed.astype(BF16)[None], (sections,) + passed.shape)
    passed = exchange(passed.reshape(sections * n_x, tok, cols), ("pipe", "dp"))
    passed, grads = lax.optimization_barrier((passed, grads))
    source = (lax.axis_index("pipe") + 1) % sections
    passed = lax.dynamic_slice_in_dim(passed, source * n_x, n_x, 0)
    passed = jnp.concatenate([passed[x] for x in range(n_x)], axis=1)[None]
    return passed, grad_combine, *grads


def solution(mesh):
    row_spec = P("pipe", ("expert", "dp"), None)
    weight_spec = P("pipe", "dp", "expert")
    in_specs = (row_spec,) * 4 + (weight_spec,) * 3
    out_specs = (row_spec,) * 2 + (weight_spec,) * 3
    return jax.shard_map(body, mesh=mesh, in_specs=in_specs, out_specs=out_specs, check_vma=False)
```
